32 devices in a mesh: groups: 2 (over y), pairs: 4 (over z), sub: 2 (over x), feat: 2 (over core).
Axes of the slice: x: 2, y: 2, z: 4, core: 2. Of those that a mesh axis runs over, the one named last changes fastest.
Arguments:
- vectors: bfloat16 [64, 640, 256], P(('groups', 'pairs'), 'sub'), parts along dimension 0
- affinity: bfloat16 [64, 640, 64], P(('groups', 'pairs'), 'sub', 'feat'), parts along dimension 0, may hold values from -6 to 6
- counts: int32 [64], P('groups'), parts along dimension 0, may hold values from 1 to 640, 15360 in all
- owner_map: int32 [64], P('groups'), parts along dimension 0, may hold values from 0 to 31, as said below
- pair_table: int32 [24, 2], P(('groups', 'pairs')), parts along dimension 0, may hold values from -1 to 31, as said below
Outputs:
- smoothed: bfloat16 [64, 640, 64], P(('groups', 'pairs'), 'sub', 'feat'), parts along dimension 0
The draws below stay inside these ranges and needn't reach their ends.
There are 2 independent parts, one for each index of `groups`. The reference program is written for one: setup_inputs(seed, part) draws one part's arguments, and reference() takes and returns one part's arrays. A program takes and returns all parts, laid end to end along the dimension named above; each array names one. Nothing has to cross between parts.
Inputs may be any that keep to these rules, and one draw needn't show every extreme that they name: A permutation: block b is stored at position owner_map[b], which lies on index owner_map[b] // 8 of pairs. `pair_table`: index p of pairs holds rows p * 3 to (p + 1) * 3 - 1. A live row (a, b) names two different blocks and a is stored on that same device; live rows come first, the others are (-1, -1). No unordered pair is listed twice. The b blocks of one device's live rows are stored on different devices, none of them the device itself. A device holds 0 to 3 live rows; some device holds exactly 3 and some none.
All inputs are finite; a program needn't handle non-finite values.
Results may differ from the reference program's by a relative error of at most 0.0025.
Values may be sent and summed in bfloat16 or wider, within the bound.
A program may use at most 64 MiB of HBM per device.

```python
import math
import jax
import jax.numpy as jnp
import numpy as np
from jax import lax

E = 256
AFF = 64
BR = 640
BLK_DEV = 8
SLOTS = 3
NBLK = 32
N_PAIRS = 4


def layout_tables(key):
    base_key = jax.random.fold_in(key, 4242)
    key_list = jax.random.split(base_key, 5)
    slot_owner = jax.random.permutation(key_list[0], NBLK).astype(jnp.int32)
    owner_map = jnp.argsort(slot_owner).astype(jnp.int32)
    position = jax.random.permutation(key_list[1], N_PAIRS).astype(jnp.int32)
    device_at = jnp.argsort(position).astype(jnp.int32)
    load_at = jax.random.randint(key_list[2], (N_PAIRS,), SLOTS // 2, SLOTS + 1)
    load_at = load_at.at[0].set(SLOTS).at[1].set(0)
    device_load = load_at[position]
    slot_iota = jnp.arange(SLOTS, dtype=jnp.int32)
    place_iota = jnp.arange(N_PAIRS, dtype=jnp.int32)
    partner_pos = (place_iota[:, None] + slot_iota[None, :] + 1) % N_PAIRS
    partner_dev = device_at[partner_pos[position]]
    own_pos = jax.random.randint(key_list[3], (N_PAIRS, SLOTS), 0, BLK_DEV).astype(jnp.int32)
    far_pos = jax.random.randint(key_list[4], (N_PAIRS, SLOTS), 0, BLK_DEV).astype(jnp.int32)
    back_slot = (N_PAIRS - 2 - slot_iota).astype(jnp.int32)
    back_own = own_pos[partner_pos, back_slot[None, :]]
    back_far = far_pos[partner_pos, back_slot[None, :]]
    offset = slot_iota + 1
    later = (2 * offset[None, :] > N_PAIRS) | (2 * offset[None, :] == N_PAIRS) & (2 * place_iota[:, None] < N_PAIRS)
    clash = later & (back_own == far_pos) & (back_far == own_pos)
    far_pos = jnp.where(clash, (far_pos + 1) % BLK_DEV, far_pos)
    own_local = own_pos[position]
    far_local = far_pos[position]
    device_iota = jnp.arange(N_PAIRS, dtype=jnp.int32)
    first_ids = slot_owner[device_iota[:, None] * BLK_DEV + own_local]
    second_ids = slot_owner[partner_dev * BLK_DEV + far_local]
    is_live = slot_iota[None, :] < device_load[:, None]
    pair_rows = jnp.stack([jnp.where(is_live, first_ids, -1), jnp.where(is_live, second_ids, -1)], axis=-1)
    return (owner_map, pair_rows.reshape(N_PAIRS * SLOTS, 2).astype(jnp.int32))


def draw_owner_map(key, part):
    return layout_tables(key)[0]


def draw_pair_table(key, part):
    return layout_tables(key)[1]


def draw_vectors(key, part):
    key = jax.random.fold_in(key, 17)
    key_list = jax.random.split(key, 4)
    picks = jax.random.randint(key_list[0], (NBLK, BR), 0, BR)
    share = jax.random.uniform(key_list[1], (NBLK, BR, 1), jnp.float32, 0.55, 0.9)
    centers = jax.random.normal(key_list[2], (BR, E), jnp.float32)
    noise = jax.random.normal(key_list[3], (NBLK, BR, E), jnp.float32)
    return (jnp.sqrt(share) * jnp.take(centers, picks, axis=0) + jnp.sqrt(1.0 - share) * noise).astype(jnp.bfloat16)


def steps_of(own_key, dims, cuts, least, largest):
    loudness = 1.0
    for axis_at, parts in cuts:
        steps = jax.random.uniform(jax.random.fold_in(jax.random.fold_in(own_key, 6), axis_at), (parts,), jnp.float32, least / len(cuts), largest / len(cuts))
        loudness = loudness * jnp.repeat(jnp.exp(steps), dims[axis_at] // parts).reshape((-1,) + (1,) * (len(dims) - 1 - axis_at))
    return loudness


def split_up(number_of, total, limit, slope):
    portions = [(1 << 20) // math.isqrt(rank ** slope) + 1 for rank in range(2, number_of + 1)]
    spare, given = total - limit - (number_of - 1), [1] * (number_of - 1)
    while spare > 0:
        free = [i for i in range(number_of - 1) if given[i] < limit]
        mass, budget = sum([portions[i] for i in free]), spare
        for i in free:
            addition = min(limit - given[i], max(1, budget * portions[i] // mass), spare)
            given[i] = given[i] + addition
            spare = spare - addition
    return np.array([limit] + given)


def ragged_sizes(stream_key, number_of, total, most, skew):
    if number_of == 2:
        one = jax.random.randint(stream_key, (), max(1, total - most), min(most, total - 1) + 1)
        return jnp.stack([one, total - one])
    tallies = jnp.asarray(split_up(number_of, total, most, skew), jnp.int32)
    couples = (number_of - 1) // 2
    source_of, receiver = tallies[1:1 + 2 * couples:2], tallies[2:2 + 2 * couples:2]
    room = jnp.minimum(source_of - 1, most - receiver)
    shifted = jax.random.randint(jax.random.fold_in(stream_key, 1), (couples,), 0, 1 << 20) % (room + 1)
    tallies = tallies.at[1:1 + 2 * couples:2].set(source_of - shifted).at[2:2 + 2 * couples:2].set(receiver + shifted)
    return tallies[jax.random.permutation(jax.random.fold_in(stream_key, 2), number_of)]


def normal_values(key, shape, deviation, bound, pieces=(), kind=jnp.bfloat16):
    entries = jax.random.normal(key, shape, jnp.float32) * deviation
    if len(pieces) > 0:
        entries = steps_of(key, shape, pieces, -0.22, 0.18) * entries
    return jnp.clip(entries, min=-bound, max=bound).astype(kind)


def setup_inputs(seed: int = 0, part: int = 0) -> dict:
    splits = jax.random.split(jax.random.key(seed), 6)
    part_keys = jax.random.split(jax.random.fold_in(splits[5], part), 6)
    return {
        "vectors": draw_vectors(jax.random.fold_in(jax.random.fold_in(splits[5], part), 71), part),
        "affinity": normal_values(part_keys[1], (NBLK, BR, AFF), 1.0, 6.0, ((0, 4), (1, 2), (2, 2))),
        "counts": ragged_sizes(part_keys[2], NBLK, NBLK * BR * 3 // 4, BR, 1).astype(jnp.int32),
        "owner_map": draw_owner_map(jax.random.fold_in(jax.random.fold_in(splits[5], part), 71), part),
        "pair_table": draw_pair_table(jax.random.fold_in(jax.random.fold_in(splits[5], part), 71), part),
    }


sharpness = 8.0

def unit_rows(vectors):
    floats = vectors.astype(jnp.float32)
    scaled = floats * lax.rsqrt(lax.optimization_barrier(jnp.sum(floats * floats, axis=-1, keepdims=True)) + 1e-06)
    return scaled.astype(jnp.bfloat16)

def reference(vectors, affinity, counts, owner_map, pair_table):
    units = unit_rows(vectors)
    slot_counts = jnp.zeros_like(counts).at[owner_map].set(counts)
    row_iota = jnp.arange(vectors.shape[1], dtype=jnp.int32)
    numer = affinity.astype(jnp.float32)
    denom = jnp.ones(vectors.shape[:2], jnp.float32)

    def one_pair(totals, table_row):
        first_id = jnp.maximum(table_row[0], 0).astype(jnp.int32)
        second_id = jnp.maximum(table_row[1], 0).astype(jnp.int32)
        first_slot = owner_map[first_id]
        second_slot = owner_map[second_id]

        def pair_work(state_in):
            numer_acc, denom_acc = state_in
            cosine = jnp.dot(units[first_slot], units[second_slot].T, preferred_element_type=jnp.float32)
            keep_mask = (row_iota < counts[first_id])[:, None] & (row_iota < counts[second_id])[None, :]
            kernel = jnp.where(keep_mask, jnp.exp(sharpness * (cosine - 1.0)), 0.0)
            rounded = kernel.astype(jnp.bfloat16)
            to_first = jnp.dot(rounded, affinity[second_slot], preferred_element_type=jnp.float32)
            to_second = jnp.dot(rounded.T, affinity[first_slot], preferred_element_type=jnp.float32)
            numer_acc = numer_acc.at[first_slot].add(to_first).at[second_slot].add(to_second)
            denom_acc = denom_acc.at[first_slot].add(lax.optimization_barrier(jnp.sum(kernel, axis=1))).at[second_slot].add(lax.optimization_barrier(jnp.sum(kernel, axis=0)))
            return (numer_acc, denom_acc)

        def pass_on(state_in):
            return state_in
        return (lax.cond(table_row[1] >= 0, pair_work, pass_on, totals), None)
    (numer, denom), ignored = lax.scan(one_pair, (numer, denom), pair_table)
    is_live = row_iota[None, :] < slot_counts[:, None]
    return jnp.where(is_live[..., None], numer / denom[..., None], 0.0).astype(jnp.bfloat16)
```

```python
import functools

import jax
import jax.numpy as jnp
from jax import lax
from jax.experimental import pallas as pl
from jax.experimental.pallas import tpu as pltpu
from jax.sharding import PartitionSpec as P

sharpness = 8.0
MESH = pl.DeviceIdType.MESH


def loop(count, body, unrolled=4):
    if count <= unrolled:
        for i in range(count):
            body(i)
    else:

        def step(i, carry):
            body(i)
            return carry

        lax.fori_loop(0, count, step, 0)


def fold(count, body, start, unrolled=4):
    if count <= unrolled:
        for i in range(count):
            start = body(i, start)
        return start
    return lax.fori_loop(0, count, body, start)


def kernel(
    pair_count,
    sub_count,
    vec_ref,
    aff_ref,
    counts_ref,
    owner_ref,
    table_ref,
    table_vec_ref,
    out_ref,
    own_units,
    own_aug,
    far_units,
    far_aug,
    send_units,
    send_aug,
    got_units,
    got_aug,
    near_send,
    near_got,
    back_own,
    back_send,
    back_got,
    tables_vec,
    tables,
    tab_send_sem,
    tab_got_sem,
    tab_local_sem,
    sub_send_sem,
    sub_got_sem,
    pair_send_sem,
    pair_got_sem,
    near_send_sem,
    near_got_sem,
    back_send_sem,
    back_got_sem,
):
    me = lax.axis_index("pairs")
    sub = lax.axis_index("sub")
    blocks, rows, _ = vec_ref.shape
    cols = aff_ref.shape[1]
    height = own_aug.shape[1]
    slots = table_ref.shape[1]
    peers = pair_count - 1
    others = sub_count - 1

    def peer_of(e):
        return lax.rem(me + e + 1, pair_count)

    def sub_of(u):
        return lax.rem(sub + u + 1, sub_count)

    def place(block):
        return owner_ref[jnp.maximum(block, 0)]

    def find(entry, target):
        def step(k, found):
            first, second = entry(0, k), entry(1, k)
            hit = (second >= 0) & (lax.div(place(second), jnp.int32(blocks)) == target)
            return jnp.where(hit, first, found[0]), jnp.where(hit, second, found[1])

        return fold(slots, step, (jnp.int32(-1), jnp.int32(-1)))

    def local_of(block):
        return lax.rem(place(block), jnp.int32(blocks))

    def own_pair(e):
        return find(lambda i, k: table_ref[i, k], peer_of(e))

    def asked_pair(e):
        return find(lambda i, k: tables[e, i, k], me)

    def fill(block, units_ref, aug_ref, e):
        floats = vec_ref[block].astype(jnp.float32)
        scale = lax.rsqrt(jnp.sum(floats * floats, axis=1, keepdims=True) + 1e-06)
        units_ref[e] = (floats * scale).astype(jnp.bfloat16)
        aug_ref[e, 0:cols, :] = aff_ref[block]
        aug_ref[e, cols:height, :] = jnp.ones((height - cols, rows), jnp.bfloat16)

    def remote(src, dst, send_sem, got_sem, device):
        return pltpu.make_async_remote_copy(
            src_ref=src,
            dst_ref=dst,
            send_sem=send_sem,
            recv_sem=got_sem,
            device_id=device,
            device_id_type=MESH,
        )

    def table_copy(e):
        there = peers - 1 - e
        return remote(
            table_vec_ref,
            tables_vec.at[there],
            tab_send_sem.at[e],
            tab_got_sem.at[there],
            {"pairs": peer_of(e)},
        )

    def sub_copies(e, u):
        there = others - 1 - u
        to = {"sub": sub_of(u)}
        return (
            remote(
                own_units.at[e],
                far_units.at[there, e],
                sub_send_sem.at[0, u, e],
                sub_got_sem.at[0, there, e],
                to,
            ),
            remote(
                own_aug.at[e],
                far_aug.at[there, e],
                sub_send_sem.at[1, u, e],
                sub_got_sem.at[1, there, e],
                to,
            ),
        )

    def pair_copies(e):
        there = peers - 1 - e
        to = {"pairs": peer_of(e)}
        return (
            remote(
                send_units.at[e],
                got_units.at[there],
                pair_send_sem.at[0, e],
                pair_got_sem.at[0, there],
                to,
            ),
            remote(
                send_aug.at[e],
                got_aug.at[there],
                pair_send_sem.at[1, e],
                pair_got_sem.at[1, there],
                to,
            ),
        )

    def near_copy(e):
        there = peers - 1 - e
        return remote(
            near_send.at[e],
            near_got.at[there],
            near_send_sem.at[e],
            near_got_sem.at[there],
            {"pairs": peer_of(e)},
        )

    def back_copy(e, u):
        there = others - 1 - u
        return remote(
            back_send.at[u, e],
            back_got.at[there, e],
            back_send_sem.at[u, e],
            back_got_sem.at[there, e],
            {"sub": sub_of(u)},
        )

    barrier = pltpu.get_barrier_semaphore()

    def greet_peer(e):
        pl.semaphore_signal(barrier, inc=1, device_id={"pairs": peer_of(e)}, device_id_type=MESH)

    def greet_sub(u):
        pl.semaphore_signal(barrier, inc=1, device_id={"sub": sub_of(u)}, device_id_type=MESH)

    loop(peers, greet_peer)
    loop(others, greet_sub)
    pl.semaphore_wait(barrier, peers + others)

    loop(peers, lambda e: table_copy(e).start())

    def start_own(e):
        fill(local_of(own_pair(e)[0]), own_units, own_aug, e)

        def send(u):
            for copy in sub_copies(e, u):
                copy.start()

        loop(others, send)

    loop(peers, start_own)

    def table_in(e):
        table_copy(peers - 1 - e).wait_recv()

    loop(peers, table_in)
    to_scalars = pltpu.make_async_copy(tables_vec, tables, tab_local_sem)
    to_scalars.start()
    to_scalars.wait()

    def start_pair(e):
        fill(local_of(asked_pair(e)[1]), send_units, send_aug, e)
        for copy in pair_copies(e):
            copy.start()

    loop(peers, start_pair)

    lane = lax.broadcasted_iota(jnp.int32, (height, rows), 1)

    def cut(aug, first_row, count):
        keep = first_row + lane < count
        return jnp.where(keep, aug.astype(jnp.float32), 0.0).astype(jnp.bfloat16)

    def tile(a_units, a_aug, b_units, b_aug):
        cosine = lax.dot_general(
            b_units, a_units, (((1,), (1,)), ((), ())), preferred_element_type=jnp.float32
        )
        rounded = jnp.exp(sharpness * (cosine - 1.0)).astype(jnp.bfloat16)
        near = lax.dot_general(
            a_aug, rounded, (((1,), (1,)), ((), ())), preferred_element_type=jnp.float32
        )
        back = jnp.dot(b_aug, rounded, preferred_element_type=jnp.float32)
        return near, back

    def pair_step(e):
        first, second = own_pair(e)
        live = second >= 0
        a_count = jnp.where(live, counts_ref[jnp.maximum(first, 0)], 0)
        b_count = jnp.where(live, counts_ref[jnp.maximum(second, 0)], 0)
        for copy in pair_copies(peers - 1 - e):
            copy.wait_recv()
        b_units = got_units[e]
        b_aug = cut(got_aug[e], sub * rows, b_count)
        near, back = tile(own_units[e], cut(own_aug[e], sub * rows, a_count), b_units, b_aug)
        back_own[e] = back
        for u in range(others):
            for copy in sub_copies(e, others - 1 - u):
                copy.wait_recv()
            more, back = tile(
                far_units[u, e], cut(far_aug[u, e], sub_of(u) * rows, a_count), b_units, b_aug
            )
            near = near + more
            back_send[u, e] = back.astype(jnp.bfloat16)
            back_copy(e, u).start()
        near_send[e] = near.astype(jnp.bfloat16)
        near_copy(e).start()

    loop(peers, pair_step)

    def count_step(b, found):
        at = owner_ref[b] - me * blocks
        return tuple(jnp.where(at == l, counts_ref[b], found[l]) for l in range(blocks))

    own_counts = fold(
        counts_ref.shape[0], count_step, (jnp.int32(0),) * blocks, unrolled=32
    )

    def arrive(e):
        near_copy(peers - 1 - e).wait_recv()

        def back_in(u):
            back_copy(e, others - 1 - u).wait_recv()

        loop(others, back_in)

    loop(peers, arrive)

    column = lax.broadcasted_iota(jnp.int32, (cols, rows), 1)
    for l in range(blocks):

        def add(e, total, l=l):
            own, asked = own_pair(e), asked_pair(e)
            mine = (own[1] >= 0) & (local_of(own[0]) == l)
            theirs = (asked[1] >= 0) & (local_of(asked[1]) == l)
            part = back_own[e]
            for u in range(others):
                part = part + back_got[u, e].astype(jnp.float32)
            total = total + jnp.where(mine, part, 0.0)
            return total + jnp.where(theirs, near_got[e].astype(jnp.float32), 0.0)

        total = fold(peers, add, jnp.zeros((height, rows), jnp.float32))
        numer = aff_ref[l].astype(jnp.float32) + total[0:cols]
        denom = 1.0 + total[cols : cols + 1]
        keep = sub * rows + column < own_counts[l]
        out_ref[l] = jnp.where(keep, numer / denom, 0.0).astype(jnp.bfloat16)

    def sent(e):
        table_copy(e).wait_send()
        near_copy(e).wait_send()
        for copy in pair_copies(e):
            copy.wait_send()

        def sub_sent(u):
            back_copy(e, u).wait_send()
            for copy in sub_copies(e, u):
                copy.wait_send()

        loop(others, sub_sent)

    loop(peers, sent)


def on_device(vectors, affinity, counts, owner_map, pair_table):
    pair_count = lax.axis_size("pairs")
    sub_count = lax.axis_size("sub")
    blocks, rows, width = vectors.shape
    cols = affinity.shape[2]
    height = cols + 16
    peers, others = pair_count - 1, sub_count - 1
    slots = pair_table.shape[0]
    table = pair_table.T
    half = jnp.bfloat16
    dma = pltpu.SemaphoreType.DMA
    vmem = pl.BlockSpec(memory_space=pltpu.VMEM)
    smem = pl.BlockSpec(memory_space=pltpu.SMEM)
    out = pl.pallas_call(
        functools.partial(kernel, pair_count, sub_count),
        out_shape=jax.ShapeDtypeStruct((blocks, cols, rows), half),
        in_specs=[vmem, vmem, smem, smem, smem, vmem],
        out_specs=vmem,
        scratch_shapes=[
            pltpu.VMEM((peers, rows, width), half),
            pltpu.VMEM((peers, height, rows), half),
            pltpu.VMEM((others, peers, rows, width), half),
            pltpu.VMEM((others, peers, height, rows), half),
            pltpu.VMEM((peers, rows, width), half),
            pltpu.VMEM((peers, height, rows), half),
            pltpu.VMEM((peers, rows, width), half),
            pltpu.VMEM((peers, height, rows), half),
            pltpu.VMEM((peers, height, rows), half),
            pltpu.VMEM((peers, height, rows), half),
            pltpu.VMEM((peers, height, rows), jnp.float32),
            pltpu.VMEM((others, peers, height, rows), half),
            pltpu.VMEM((others, peers, height, rows), half),
            pltpu.VMEM((peers, 2, slots), jnp.int32),
            pltpu.SMEM((peers, 2, slots), jnp.int32),
            dma((peers,)),
            dma((peers,)),
            dma(()),
            dma((2, others, peers)),
            dma((2, others, peers)),
            dma((2, peers)),
            dma((2, peers)),
            dma((peers,)),
            dma((peers,)),
            dma((others, peers)),
            dma((others, peers)),
        ],
        compiler_params=pltpu.CompilerParams(
            collective_id=0, has_side_effects=True, vmem_limit_bytes=50 * 1024 * 1024
        ),
        name="pair_sums",
    )(vectors, affinity.transpose(0, 2, 1), counts, owner_map, table, table)
    return out.transpose(0, 2, 1)


def solution(mesh):
    in_specs = (
        P(("groups", "pairs"), "sub", None),
        P(("groups", "pairs"), "sub", "feat"),
        P("groups"),
        P("groups"),
        P(("groups", "pairs"), None),
    )
    out_specs = P(("groups", "pairs"), "sub", "feat")
    return jax.shard_map(
        on_device, mesh=mesh, in_specs=in_specs, out_specs=out_specs, check_vma=False
    )
```

```python
import functools

import jax
import jax.numpy as jnp
from jax import lax
from jax.experimental import pallas as pl
from jax.experimental.pallas import tpu as pltpu
from jax.sharding import PartitionSpec as P

sharpness = 8.0
MESH = pl.DeviceIdType.MESH


def loop(count, body, unrolled=4):
    if count <= unrolled:
        for i in range(count):
            body(i)
    else:

        def step(i, carry):
            body(i)
            return carry

        lax.fori_loop(0, count, step, 0)


def fold(count, body, start, unrolled=4):
    if count <= unrolled:
        for i in range(count):
            start = body(i, start)
        return start
    return lax.fori_loop(0, count, body, start)


def kernel(
    pair_count,
    sub_count,
    core_count,
    vec_hbm,
    aff_hbm,
    counts_hbm,
    owner_hbm,
    table_hbm,
    out_ref,
    vec_ref,
    aff_ref,
    counts_ref,
    owner_ref,
    table_ref,
    own_units,
    own_aug,
    far_units,
    far_aug,
    send_units,
    send_aug,
    got_units,
    got_aug,
    near_send,
    near_got,
    back_own,
    back_send,
    back_got,
    tables_vec,
    tables,
    fetch_sem,
    tab_send_sem,
    tab_got_sem,
    tab_local_sem,
    sub_send_sem,
    sub_got_sem,
    pair_send_sem,
    pair_got_sem,
    near_send_sem,
    near_got_sem,
    back_send_sem,
    back_got_sem,
    far_send_sem,
    far_got_sem,
    share_send_sem,
    share_got_sem,
):
    me = lax.axis_index("pairs")
    sub = lax.axis_index("sub")
    core = lax.axis_index("feat")
    blocks, _, part, width = vec_ref.shape
    rows = part * core_count
    cols = aff_ref.shape[1]
    mates = core_count - 1
    height = own_aug.shape[1]
    slots = table_ref.shape[1]
    peers = pair_count - 1
    others = sub_count - 1

    def peer_of(e):
        return lax.rem(me + e + 1, pair_count)

    def sub_of(u):
        return lax.rem(sub + u + 1, sub_count)

    def place(block):
        return owner_ref[jnp.maximum(block, 0)]

    def find(entry, target):
        def step(k, found):
            first, second = entry(0, k), entry(1, k)
            hit = (second >= 0) & (lax.div(place(second), jnp.int32(blocks)) == target)
            return jnp.where(hit, first, found[0]), jnp.where(hit, second, found[1])

        return fold(slots, step, (jnp.int32(-1), jnp.int32(-1)))

    def local_of(block):
        return lax.rem(place(block), jnp.int32(blocks))

    def mate_of(v):
        return lax.rem(core + v + 1, core_count)

    known = {}

    def once(name, e, work):
        if not isinstance(e, int):
            return work()
        if (name, e) not in known:
            known[name, e] = work()
        return known[name, e]

    def own_pair(e):
        return once("own", e, lambda: find(lambda i, k: table_ref[i, k], peer_of(e)))

    def asked_pair(e):
        return once("asked", e, lambda: find(lambda i, k: tables[e, i, k], me))

    def own_local(e):
        return once("own at", e, lambda: local_of(own_pair(e)[0]))

    def asked_local(e):
        return once("asked at", e, lambda: local_of(asked_pair(e)[1]))

    def unit(floats):
        floats = floats.astype(jnp.float32)
        scale = lax.rsqrt(jnp.sum(floats * floats, axis=1, keepdims=True) + 1e-06)
        return (floats * scale).astype(jnp.bfloat16)

    def fill_aug(block, aug_ref, e):
        aug_ref[e, 0:cols, :] = aff_ref[block]
        aug_ref[e, cols:height, :] = jnp.ones((height - cols, rows), jnp.bfloat16)

    def remote(src, dst, send_sem, got_sem, device):
        return pltpu.make_async_remote_copy(
            src_ref=src,
            dst_ref=dst,
            send_sem=send_sem,
            recv_sem=got_sem,
            device_id=device,
            device_id_type=MESH,
        )

    def table_copy(e):
        there = peers - 1 - e
        return remote(
            table_hbm,
            tables_vec.at[there],
            tab_send_sem.at[e],
            tab_got_sem.at[there],
            {"pairs": peer_of(e)},
        )

    def sub_copies(e, u):
        there = others - 1 - u
        to = {"sub": sub_of(u)}
        return (
            remote(
                own_units.at[e, core],
                far_units.at[there, e, core],
                sub_send_sem.at[0, u, e],
                sub_got_sem.at[0, there, e],
                to,
            ),
            remote(
                own_aug.at[e],
                far_aug.at[there, e],
                sub_send_sem.at[1, u, e],
                sub_got_sem.at[1, there, e],
                to,
            ),
        )

    def pair_copies(e):
        there = peers - 1 - e
        to = {"pairs": peer_of(e)}
        return (
            remote(
                send_units.at[e],
                got_units.at[there, core],
                pair_send_sem.at[0, e],
                pair_got_sem.at[0, there],
                to,
            ),
            remote(
                send_aug.at[e],
                got_aug.at[there],
                pair_send_sem.at[1, e],
                pair_got_sem.at[1, there],
                to,
            ),
        )

    def far_share(e, u, v):
        there = mates - 1 - v
        piece = far_units.at[u, e, core]
        return remote(
            piece,
            piece,
            far_send_sem.at[u, e, v],
            far_got_sem.at[u, e, there],
            {"feat": mate_of(v)},
        )

    def got_share(e, v):
        there = mates - 1 - v
        piece = got_units.at[e, core]
        return remote(
            piece,
            piece,
            share_send_sem.at[e, v],
            share_got_sem.at[e, there],
            {"feat": mate_of(v)},
        )

    def near_copy(e):
        there = peers - 1 - e
        return remote(
            near_send.at[e],
            near_got.at[there],
            near_send_sem.at[e],
            near_got_sem.at[there],
            {"pairs": peer_of(e)},
        )

    def back_copy(e, u):
        there = others - 1 - u
        return remote(
            back_send.at[u, e],
            back_got.at[there, e],
            back_send_sem.at[u, e],
            back_got_sem.at[there, e],
            {"sub": sub_of(u)},
        )

    fetches = [
        pltpu.make_async_copy(src, dst, fetch_sem.at[i])
        for i, (src, dst) in enumerate(
            [
                (table_hbm, table_ref),
                (owner_hbm, owner_ref),
                (counts_hbm, counts_ref),
                (vec_hbm, vec_ref),
                (aff_hbm, aff_ref),
            ]
        )
    ]
    for fetch in fetches:
        fetch.start()

    barrier = pltpu.get_barrier_semaphore()

    def greet_peer(e):
        pl.semaphore_signal(barrier, inc=1, device_id={"pairs": peer_of(e)}, device_id_type=MESH)

    def greet_sub(u):
        pl.semaphore_signal(barrier, inc=1, device_id={"sub": sub_of(u)}, device_id_type=MESH)

    loop(peers, greet_peer)
    def greet_mate(v):
        pl.semaphore_signal(barrier, inc=1, device_id={"feat": mate_of(v)}, device_id_type=MESH)

    loop(others, greet_sub)
    loop(mates, greet_mate)
    pl.semaphore_wait(barrier, peers + others + mates)

    loop(peers, lambda e: table_copy(e).start())
    for fetch in fetches:
        fetch.wait()

    def start_own(e):
        own_units[e] = unit(vec_ref[own_local(e)].reshape(rows, width)).reshape(
            core_count, part, width
        )
        fill_aug(own_local(e), own_aug, e)

        def send(u):
            for copy in sub_copies(e, u):
                copy.start()

        loop(others, send)

    loop(peers, start_own)

    def table_in(e):
        table_copy(peers - 1 - e).wait_recv()

    loop(peers, table_in)
    to_scalars = pltpu.make_async_copy(tables_vec, tables, tab_local_sem)
    to_scalars.start()
    to_scalars.wait()

    def start_pair(e):
        send_units[e] = unit(vec_ref[asked_local(e), core])
        fill_aug(asked_local(e), send_aug, e)
        for copy in pair_copies(e):
            copy.start()

    loop(peers, start_pair)

    def count_step(b, found):
        at = owner_ref[b] - me * blocks
        return tuple(jnp.where(at == l, counts_ref[b], found[l]) for l in range(blocks))

    own_counts = fold(
        counts_ref.shape[0], count_step, (jnp.int32(0),) * blocks, unrolled=32
    )

    def share_far(e):
        for u in range(others):
            for copy in sub_copies(e, others - 1 - u):
                copy.wait_recv()
            for v in range(mates):
                far_share(e, u, v).start()

    def share_got(e):
        for copy in pair_copies(peers - 1 - e):
            copy.wait_recv()
        for v in range(mates):
            got_share(e, v).start()

    loop(peers, share_far)
    loop(peers, share_got)

    lane = lax.broadcasted_iota(jnp.int32, (height, rows), 1)

    def cut(aug, first_row, count):
        keep = first_row + lane < count
        return jnp.where(keep, aug.astype(jnp.float32), 0.0).astype(jnp.bfloat16)

    def tile(a_units, a_aug, b_units, b_aug):
        cosine = lax.dot_general(
            b_units, a_units, (((1,), (1,)), ((), ())), preferred_element_type=jnp.float32
        )
        rounded = jnp.exp(sharpness * (cosine - 1.0)).astype(jnp.bfloat16)
        near = lax.dot_general(
            a_aug, rounded, (((1,), (1,)), ((), ())), preferred_element_type=jnp.float32
        )
        back = jnp.dot(b_aug, rounded, preferred_element_type=jnp.float32)
        return near, back

    def pair_step(e):
        first, second = own_pair(e)
        live = second >= 0
        a_count = jnp.where(live, counts_ref[jnp.maximum(first, 0)], 0)
        b_count = jnp.where(live, counts_ref[jnp.maximum(second, 0)], 0)
        for v in range(mates):
            got_share(e, mates - 1 - v).wait_recv()
        b_units = got_units[e].reshape(rows, width)
        b_aug = cut(got_aug[e], sub * rows, b_count)
        near, back = tile(
            own_units[e].reshape(rows, width), cut(own_aug[e], sub * rows, a_count), b_units, b_aug
        )
        back_own[e] = back
        for u in range(others):
            for v in range(mates):
                far_share(e, u, mates - 1 - v).wait_recv()
            more, back = tile(
                far_units[u, e].reshape(rows, width),
                cut(far_aug[u, e], sub_of(u) * rows, a_count),
                b_units,
                b_aug,
            )
            near = near + more
            back_send[u, e] = back.astype(jnp.bfloat16)
            back_copy(e, u).start()
        near_send[e] = near.astype(jnp.bfloat16)
        near_copy(e).start()

    loop(peers, pair_step)

    def arrive(e):
        near_copy(peers - 1 - e).wait_recv()

        def back_in(u):
            back_copy(e, others - 1 - u).wait_recv()

        loop(others, back_in)

    loop(peers, arrive)

    column = lax.broadcasted_iota(jnp.int32, (cols, rows), 1)
    for l in range(blocks):

        def add(e, total, l=l):
            own, asked = own_pair(e), asked_pair(e)
            mine = (own[1] >= 0) & (own_local(e) == l)
            theirs = (asked[1] >= 0) & (asked_local(e) == l)
            part = back_own[e]
            for u in range(others):
                part = part + back_got[u, e].astype(jnp.float32)
            total = total + jnp.where(mine, part, 0.0)
            return total + jnp.where(theirs, near_got[e].astype(jnp.float32), 0.0)

        total = fold(peers, add, jnp.zeros((height, rows), jnp.float32))
        numer = aff_ref[l].astype(jnp.float32) + total[0:cols]
        denom = 1.0 + total[cols : cols + 1]
        keep = sub * rows + column < own_counts[l]
        out_ref[l] = jnp.where(keep, numer * (1.0 / denom), 0.0).astype(jnp.bfloat16)

    def sent(e):
        table_copy(e).wait_send()
        near_copy(e).wait_send()
        for copy in pair_copies(e):
            copy.wait_send()
        for v in range(mates):
            got_share(e, v).wait_send()

        def sub_sent(u):
            for v in range(mates):
                far_share(e, u, v).wait_send()
            back_copy(e, u).wait_send()
            for copy in sub_copies(e, u):
                copy.wait_send()

        loop(others, sub_sent)

    loop(peers, sent)


def on_device(vectors, affinity, counts, owner_map, pair_table):
    pair_count = lax.axis_size("pairs")
    sub_count = lax.axis_size("sub")
    core_count = lax.axis_size("feat")
    blocks, rows, width = vectors.shape
    cols = affinity.shape[2]
    height = cols + 16
    peers, others, mates = pair_count - 1, sub_count - 1, core_count - 1
    part = rows // core_count
    parts = (core_count, part, width)
    slots = pair_table.shape[0]
    table = pair_table.T
    half = jnp.bfloat16
    dma = pltpu.SemaphoreType.DMA
    vmem = pl.BlockSpec(memory_space=pltpu.VMEM)
    hbm = pl.BlockSpec(memory_space=pltpu.HBM)
    out = pl.pallas_call(
        functools.partial(kernel, pair_count, sub_count, core_count),
        out_shape=jax.ShapeDtypeStruct((blocks, cols, rows), half),
        in_specs=[hbm] * 5,
        out_specs=vmem,
        scratch_shapes=[
            pltpu.VMEM((blocks,) + parts, half),
            pltpu.VMEM((blocks, cols, rows), half),
            pltpu.SMEM(counts.shape, jnp.int32),
            pltpu.SMEM(owner_map.shape, jnp.int32),
            pltpu.SMEM((2, slots), jnp.int32),
            pltpu.VMEM((peers,) + parts, half),
            pltpu.VMEM((peers, height, rows), half),
            pltpu.VMEM((others, peers) + parts, half),
            pltpu.VMEM((others, peers, height, rows), half),
            pltpu.VMEM((peers, part, width), half),
            pltpu.VMEM((peers, height, rows), half),
            pltpu.VMEM((peers,) + parts, half),
            pltpu.VMEM((peers, height, rows), half),
            pltpu.VMEM((peers, height, rows), half),
            pltpu.VMEM((peers, height, rows), half),
            pltpu.VMEM((peers, height, rows), jnp.float32),
            pltpu.VMEM((others, peers, height, rows), half),
            pltpu.VMEM((others, peers, height, rows), half),
            pltpu.VMEM((peers, 2, slots), jnp.int32),
            pltpu.SMEM((peers, 2, slots), jnp.int32),
            dma((5,)),
            dma((peers,)),
            dma((peers,)),
            dma(()),
            dma((2, others, peers)),
            dma((2, others, peers)),
            dma((2, peers)),
            dma((2, peers)),
            dma((peers,)),
            dma((peers,)),
            dma((others, peers)),
            dma((others, peers)),
            dma((others, peers, mates)),
            dma((others, peers, mates)),
            dma((peers, mates)),
            dma((peers, mates)),
        ],
        compiler_params=pltpu.CompilerParams(
            collective_id=0, has_side_effects=True, vmem_limit_bytes=62 * 1024 * 1024
        ),
        name="pair_sums",
    )(
        vectors.reshape((blocks,) + parts),
        affinity.transpose(0, 2, 1),
        counts,
        owner_map,
        table,
    )
    return out.transpose(0, 2, 1)


def solution(mesh):
    in_specs = (
        P(("groups", "pairs"), "sub", None),
        P(("groups", "pairs"), "sub", "feat"),
        P("groups"),
        P("groups"),
        P(("groups", "pairs"), None),
    )
    out_specs = P(("groups", "pairs"), "sub", "feat")
    return jax.shard_map(
        on_device, mesh=mesh, in_specs=in_specs, out_specs=out_specs, check_vma=False
    )
```

```python
import functools

import jax
import jax.numpy as jnp
from jax import lax
from jax.experimental import pallas as pl
from jax.experimental.pallas import tpu as pltpu
from jax.sharding import PartitionSpec as P

sharpness = 8.0
MESH = pl.DeviceIdType.MESH


def loop(count, body, unrolled=4):
    if count <= unrolled:
        for i in range(count):
            body(i)
    else:

        def step(i, carry):
            body(i)
            return carry

        lax.fori_loop(0, count, step, 0)


def fold(count, body, start, unrolled=4):
    if count <= unrolled:
        for i in range(count):
            start = body(i, start)
        return start
    return lax.fori_loop(0, count, body, start)


def kernel(
    pair_count,
    sub_count,
    core_count,
    vec_hbm,
    aff_hbm,
    counts_hbm,
    owner_hbm,
    table_hbm,
    out_ref,
    vec_ref,
    aff_ref,
    counts_ref,
    owner_ref,
    table_ref,
    own_units,
    own_aff,
    far_units,
    far_aff,
    send_units,
    send_aff,
    got_units,
    got_aff,
    near_send,
    near_got,
    back_own,
    back_send,
    back_got,
    tables_vec,
    tables,
    fetch_sem,
    tab_send_sem,
    tab_got_sem,
    tab_local_sem,
    sub_send_sem,
    sub_got_sem,
    pair_send_sem,
    pair_got_sem,
    near_send_sem,
    near_got_sem,
    back_send_sem,
    back_got_sem,
    far_send_sem,
    far_got_sem,
    share_send_sem,
    share_got_sem,
):
    me = lax.axis_index("pairs")
    sub = lax.axis_index("sub")
    core = lax.axis_index("feat")
    blocks, _, part, width = vec_ref.shape
    rows = part * core_count
    cols = aff_ref.shape[1]
    mates = core_count - 1
    height = back_own.shape[1]
    slots = table_ref.shape[1]
    peers = pair_count - 1
    others = sub_count - 1

    def peer_of(e):
        return lax.rem(me + e + 1, pair_count)

    def sub_of(u):
        return lax.rem(sub + u + 1, sub_count)

    def place(block):
        return owner_ref[jnp.maximum(block, 0)]

    def find(entry, target):
        def step(k, found):
            first, second = entry(0, k), entry(1, k)
            hit = (second >= 0) & (lax.div(place(second), jnp.int32(blocks)) == target)
            return jnp.where(hit, first, found[0]), jnp.where(hit, second, found[1])

        return fold(slots, step, (jnp.int32(-1), jnp.int32(-1)))

    def local_of(block):
        return lax.rem(place(block), jnp.int32(blocks))

    def mate_of(v):
        return lax.rem(core + v + 1, core_count)

    known = {}

    def once(name, e, work):
        if not isinstance(e, int):
            return work()
        if (name, e) not in known:
            known[name, e] = work()
        return known[name, e]

    def own_pair(e):
        return once("own", e, lambda: find(lambda i, k: tables[e, i, k], me)[::-1])

    def asked_pair(e):
        return once("asked", e, lambda: find(lambda i, k: table_ref[i, k], peer_of(e))[::-1])

    def own_local(e):
        return once("own at", e, lambda: local_of(own_pair(e)[0]))

    def asked_local(e):
        return once("asked at", e, lambda: local_of(asked_pair(e)[1]))

    def unit(floats):
        floats = floats.astype(jnp.float32)
        scale = lax.rsqrt(jnp.sum(floats * floats, axis=1, keepdims=True) + 1e-06)
        return (floats * scale).astype(jnp.bfloat16)

    def fill_aff(block, to_ref, e):
        to_ref[e] = aff_ref[block]

    def remote(src, dst, send_sem, got_sem, device):
        return pltpu.make_async_remote_copy(
            src_ref=src,
            dst_ref=dst,
            send_sem=send_sem,
            recv_sem=got_sem,
            device_id=device,
            device_id_type=MESH,
        )

    def table_copy(e):
        there = peers - 1 - e
        return remote(
            table_hbm,
            tables_vec.at[there],
            tab_send_sem.at[e],
            tab_got_sem.at[there],
            {"pairs": peer_of(e)},
        )

    def sub_copies(e, u):
        there = others - 1 - u
        to = {"sub": sub_of(u)}
        return (
            remote(
                own_units.at[e, core],
                far_units.at[there, e, core],
                sub_send_sem.at[0, u, e],
                sub_got_sem.at[0, there, e],
                to,
            ),
            remote(
                own_aff.at[e],
                far_aff.at[there, e],
                sub_send_sem.at[1, u, e],
                sub_got_sem.at[1, there, e],
                to,
            ),
        )

    def pair_copies(e):
        there = peers - 1 - e
        to = {"pairs": peer_of(e)}
        return (
            remote(
                send_units.at[e],
                got_units.at[there, core],
                pair_send_sem.at[0, e],
                pair_got_sem.at[0, there],
                to,
            ),
            remote(
                send_aff.at[e],
                got_aff.at[there],
                pair_send_sem.at[1, e],
                pair_got_sem.at[1, there],
                to,
            ),
        )

    def far_share(e, u, v):
        there = mates - 1 - v
        piece = far_units.at[u, e, core]
        return remote(
            piece,
            piece,
            far_send_sem.at[u, e, v],
            far_got_sem.at[u, e, there],
            {"feat": mate_of(v)},
        )

    def got_share(e, v):
        there = mates - 1 - v
        piece = got_units.at[e, core]
        return remote(
            piece,
            piece,
            share_send_sem.at[e, v],
            share_got_sem.at[e, there],
            {"feat": mate_of(v)},
        )

    def near_copy(e):
        there = peers - 1 - e
        return remote(
            near_send.at[e],
            near_got.at[there],
            near_send_sem.at[e],
            near_got_sem.at[there],
            {"pairs": peer_of(e)},
        )

    def back_copy(e, u):
        there = others - 1 - u
        return remote(
            back_send.at[u, e],
            back_got.at[there, e],
            back_send_sem.at[u, e],
            back_got_sem.at[there, e],
            {"sub": sub_of(u)},
        )

    fetches = [
        pltpu.make_async_copy(src, dst, fetch_sem.at[i])
        for i, (src, dst) in enumerate(
            [
                (table_hbm, table_ref),
                (owner_hbm, owner_ref),
                (counts_hbm, counts_ref),
                (vec_hbm, vec_ref),
                (aff_hbm, aff_ref),
            ]
        )
    ]
    for fetch in fetches:
        fetch.start()

    barrier = pltpu.get_barrier_semaphore()

    def greet_peer(e):
        pl.semaphore_signal(barrier, inc=1, device_id={"pairs": peer_of(e)}, device_id_type=MESH)

    def greet_sub(u):
        pl.semaphore_signal(barrier, inc=1, device_id={"sub": sub_of(u)}, device_id_type=MESH)

    loop(peers, greet_peer)
    def greet_mate(v):
        pl.semaphore_signal(barrier, inc=1, device_id={"feat": mate_of(v)}, device_id_type=MESH)

    loop(others, greet_sub)
    loop(mates, greet_mate)
    for fetch in fetches:
        fetch.wait()

    def fill_pair(e):
        send_units[e] = unit(vec_ref[asked_local(e), core])
        fill_aff(asked_local(e), send_aff, e)

    loop(peers, fill_pair)
    pl.semaphore_wait(barrier, peers + others + mates)

    loop(peers, lambda e: table_copy(e).start())

    def start_pair(e):
        for copy in pair_copies(e):
            copy.start()

    loop(peers, start_pair)

    loop(peers, lambda e: table_copy(peers - 1 - e).wait_recv())
    to_scalars = pltpu.make_async_copy(tables_vec, tables, tab_local_sem)
    to_scalars.start()
    to_scalars.wait()

    def start_own(e):
        own_units[e, core] = unit(vec_ref[own_local(e), core])
        fill_aff(own_local(e), own_aff, e)

        def send(u):
            for copy in sub_copies(e, u):
                copy.start()

        loop(others, send)

    loop(peers, start_own)

    def fill_rest(e):
        for v in range(mates):
            own_units[e, mate_of(v)] = unit(vec_ref[own_local(e), mate_of(v)])

    loop(peers, fill_rest)

    def count_step(b, found):
        at = owner_ref[b] - me * blocks
        return tuple(jnp.where(at == l, counts_ref[b], found[l]) for l in range(blocks))

    own_counts = fold(
        counts_ref.shape[0], count_step, (jnp.int32(0),) * blocks, unrolled=32
    )

    def share_far(e):
        for u in range(others):
            for copy in sub_copies(e, others - 1 - u):
                copy.wait_recv()
            for v in range(mates):
                far_share(e, u, v).start()

    def share_got(e):
        for copy in pair_copies(peers - 1 - e):
            copy.wait_recv()
        for v in range(mates):
            got_share(e, v).start()

    loop(peers, share_far)

    lane = lax.broadcasted_iota(jnp.int32, (height, rows), 1)

    def cut(aff, first_row, count):
        keep = first_row + lane < count
        full = jnp.concatenate(
            [aff.astype(jnp.float32), jnp.ones((height - cols, rows), jnp.float32)], axis=0
        )
        return jnp.where(keep, full, 0.0).astype(jnp.bfloat16)

    def tile(a_units, a_aug, b_units, b_aug):
        cosine = lax.dot_general(
            b_units, a_units, (((1,), (1,)), ((), ())), preferred_element_type=jnp.float32
        )
        rounded = jnp.exp(sharpness * (cosine - 1.0)).astype(jnp.bfloat16)
        near = lax.dot_general(
            a_aug, rounded, (((1,), (1,)), ((), ())), preferred_element_type=jnp.float32
        )
        back = jnp.dot(b_aug, rounded, preferred_element_type=jnp.float32)
        return near, back

    def pair_step(e):
        first, second = own_pair(e)
        live = second >= 0
        a_count = jnp.where(live, counts_ref[jnp.maximum(first, 0)], 0)
        b_count = jnp.where(live, counts_ref[jnp.maximum(second, 0)], 0)
        for v in range(mates):
            got_share(e, mates - 1 - v).wait_recv()
        b_units = got_units[e].reshape(rows, width)
        b_aug = cut(got_aff[e], sub * rows, b_count)
        near, back = tile(
            own_units[e].reshape(rows, width), cut(own_aff[e], sub * rows, a_count), b_units, b_aug
        )
        back_own[e] = back
        for u in range(others):
            for v in range(mates):
                far_share(e, u, mates - 1 - v).wait_recv()
            more, back = tile(
                far_units[u, e].reshape(rows, width),
                cut(far_aff[u, e], sub_of(u) * rows, a_count),
                b_units,
                b_aug,
            )
            near = near + more
            back_send[u, e] = back.astype(jnp.bfloat16)
            back_copy(e, u).start()
        near_send[e] = near.astype(jnp.bfloat16)
        near_copy(e).start()

    if peers > 0:
        share_got(0)

    def pair_turn(e):
        if isinstance(e, int):
            if e + 1 < peers:
                share_got(e + 1)
        else:

            @pl.when(e + 1 < peers)
            def _():
                share_got(e + 1)

        pair_step(e)

    loop(peers, pair_turn)

    def arrive(e):
        near_copy(peers - 1 - e).wait_recv()

        def back_in(u):
            back_copy(e, others - 1 - u).wait_recv()

        loop(others, back_in)

    loop(peers, arrive)

    column = lax.broadcasted_iota(jnp.int32, (cols, rows), 1)
    for l in range(blocks):

        def add(e, total, l=l):
            own, asked = own_pair(e), asked_pair(e)
            mine = (own[1] >= 0) & (own_local(e) == l)
            theirs = (asked[1] >= 0) & (asked_local(e) == l)
            part = back_own[e]
            for u in range(others):
                part = part + back_got[u, e].astype(jnp.float32)
            total = total + jnp.where(mine, part, 0.0)
            return total + jnp.where(theirs, near_got[e].astype(jnp.float32), 0.0)

        total = fold(peers, add, jnp.zeros((height, rows), jnp.float32))
        numer = aff_ref[l].astype(jnp.float32) + total[0:cols]
        denom = 1.0 + total[cols : cols + 1]
        keep = sub * rows + column < own_counts[l]
        out_ref[l] = jnp.where(keep, numer * (1.0 / denom), 0.0).astype(jnp.bfloat16)

    def sent(e):
        table_copy(e).wait_send()
        near_copy(e).wait_send()
        for copy in pair_copies(e):
            copy.wait_send()
        for v in range(mates):
            got_share(e, v).wait_send()

        def sub_sent(u):
            for v in range(mates):
                far_share(e, u, v).wait_send()
            back_copy(e, u).wait_send()
            for copy in sub_copies(e, u):
                copy.wait_send()

        loop(others, sub_sent)

    loop(peers, sent)


def on_device(vectors, affinity, counts, owner_map, pair_table):
    pair_count = lax.axis_size("pairs")
    sub_count = lax.axis_size("sub")
    core_count = lax.axis_size("feat")
    blocks, rows, width = vectors.shape
    cols = affinity.shape[2]
    height = cols + 16
    peers, others, mates = pair_count - 1, sub_count - 1, core_count - 1
    part = rows // core_count
    parts = (core_count, part, width)
    slots = pair_table.shape[0]
    table = pair_table.T
    half = jnp.bfloat16
    dma = pltpu.SemaphoreType.DMA
    vmem = pl.BlockSpec(memory_space=pltpu.VMEM)
    hbm = pl.BlockSpec(memory_space=pltpu.HBM)
    out = pl.pallas_call(
        functools.partial(kernel, pair_count, sub_count, core_count),
        out_shape=jax.ShapeDtypeStruct((blocks, cols, rows), half),
        in_specs=[hbm] * 5,
        out_specs=vmem,
        scratch_shapes=[
            pltpu.VMEM((blocks,) + parts, half),
            pltpu.VMEM((blocks, cols, rows), half),
            pltpu.SMEM(counts.shape, jnp.int32),
            pltpu.SMEM(owner_map.shape, jnp.int32),
            pltpu.SMEM((2, slots), jnp.int32),
            pltpu.VMEM((peers,) + parts, half),
            pltpu.VMEM((peers, cols, rows), half),
            pltpu.VMEM((others, peers) + parts, half),
            pltpu.VMEM((others, peers, cols, rows), half),
            pltpu.VMEM((peers, part, width), half),
            pltpu.VMEM((peers, cols, rows), half),
            pltpu.VMEM((peers,) + parts, half),
            pltpu.VMEM((peers, cols, rows), half),
            pltpu.VMEM((peers, height, rows), half),
            pltpu.VMEM((peers, height, rows), half),
            pltpu.VMEM((peers, height, rows), jnp.float32),
            pltpu.VMEM((others, peers, height, rows), half),
            pltpu.VMEM((others, peers, height, rows), half),
            pltpu.VMEM((peers, 2, slots), jnp.int32),
            pltpu.SMEM((peers, 2, slots), jnp.int32),
            dma((5,)),
            dma((peers,)),
            dma((peers,)),
            dma(()),
            dma((2, others, peers)),
            dma((2, others, peers)),
            dma((2, peers)),
            dma((2, peers)),
            dma((peers,)),
            dma((peers,)),
            dma((others, peers)),
            dma((others, peers)),
            dma((others, peers, mates)),
            dma((others, peers, mates)),
            dma((peers, mates)),
            dma((peers, mates)),
        ],
        compiler_params=pltpu.CompilerParams(
            collective_id=0, has_side_effects=True, vmem_limit_bytes=62 * 1024 * 1024
        ),
        name="pair_sums",
    )(
        vectors.reshape((blocks,) + parts),
        affinity.transpose(0, 2, 1),
        counts,
        owner_map,
        table,
    )
    return out.transpose(0, 2, 1)


def solution(mesh):
    in_specs = (
        P(("groups", "pairs"), "sub", None),
        P(("groups", "pairs"), "sub", "feat"),
        P("groups"),
        P("groups"),
        P(("groups", "pairs"), None),
    )
    out_specs = P(("groups", "pairs"), "sub", "feat")
    return jax.shard_map(
        on_device, mesh=mesh, in_specs=in_specs, out_specs=out_specs, check_vma=False
    )
```

```python
import functools

import jax
import jax.numpy as jnp
from jax import lax
from jax.experimental import pallas as pl
from jax.experimental.pallas import tpu as pltpu
from jax.sharding import PartitionSpec as P

sharpness = 8.0
MESH = pl.DeviceIdType.MESH


def loop(count, body, unrolled=4):
    if count <= unrolled:
        for i in range(count):
            body(i)
    else:

        def step(i, carry):
            body(i)
            return carry

        lax.fori_loop(0, count, step, 0)


def fold(count, body, start, unrolled=4):
    if count <= unrolled:
        for i in range(count):
            start = body(i, start)
        return start
    return lax.fori_loop(0, count, body, start)


def kernel(
    pair_count,
    sub_count,
    core_count,
    vec_hbm,
    aff_hbm,
    counts_hbm,
    owner_hbm,
    table_hbm,
    out_ref,
    vec_ref,
    aff_ref,
    counts_ref,
    owner_ref,
    table_ref,
    own_units,
    own_aff,
    far_units,
    far_aff,
    send_units,
    send_aff,
    got_units,
    got_aff,
    near_sum,
    near_send,
    near_got,
    back_own,
    back_send,
    back_got,
    tables,
    fetch_sem,
    tab_send_sem,
    tab_got_sem,
    sub_send_sem,
    sub_got_sem,
    pair_send_sem,
    pair_got_sem,
    near_send_sem,
    near_got_sem,
    back_send_sem,
    back_got_sem,
    far_send_sem,
    far_got_sem,
    share_send_sem,
    share_got_sem,
):
    me = lax.axis_index("pairs")
    sub = lax.axis_index("sub")
    core = lax.axis_index("feat")
    blocks, _, part, width = vec_ref.shape
    rows = part * core_count
    cols = aff_ref.shape[1]
    mates = core_count - 1
    height = back_own.shape[1]
    slots = table_ref.shape[1]
    peers = pair_count - 1
    others = sub_count - 1

    def peer_of(e):
        return lax.rem(me + e + 1, pair_count)

    def sub_of(u):
        return lax.rem(sub + u + 1, sub_count)

    def place(block):
        return owner_ref[jnp.maximum(block, 0)]

    def find(entry, target):
        def step(k, found):
            first, second = entry(0, k), entry(1, k)
            hit = (second >= 0) & (lax.div(place(second), jnp.int32(blocks)) == target)
            return jnp.where(hit, first, found[0]), jnp.where(hit, second, found[1])

        return fold(slots, step, (jnp.int32(-1), jnp.int32(-1)))

    def local_of(block):
        return lax.rem(place(block), jnp.int32(blocks))

    def mate_of(v):
        return lax.rem(core + v + 1, core_count)

    known = {}

    def once(name, e, work):
        if not isinstance(e, int):
            return work()
        if (name, e) not in known:
            known[name, e] = work()
        return known[name, e]

    def own_pair(e):
        return once("own", e, lambda: find(lambda i, k: tables[e, i, k], me)[::-1])

    def asked_pair(e):
        return once("asked", e, lambda: find(lambda i, k: table_ref[i, k], peer_of(e))[::-1])

    def own_local(e):
        return once("own at", e, lambda: local_of(own_pair(e)[0]))

    def asked_local(e):
        return once("asked at", e, lambda: local_of(asked_pair(e)[1]))

    def unit(floats):
        floats = floats.astype(jnp.float32)
        scale = lax.rsqrt(jnp.sum(floats * floats, axis=1, keepdims=True) + 1e-06)
        return (floats * scale).astype(jnp.bfloat16)

    def fill_aff(block, to_ref, e):
        to_ref[e] = aff_ref[block]

    def remote(src, dst, send_sem, got_sem, device):
        return pltpu.make_async_remote_copy(
            src_ref=src,
            dst_ref=dst,
            send_sem=send_sem,
            recv_sem=got_sem,
            device_id=device,
            device_id_type=MESH,
        )

    def table_copy(e):
        there = peers - 1 - e
        return remote(
            table_ref,
            tables.at[there],
            tab_send_sem.at[e],
            tab_got_sem.at[there],
            {"pairs": peer_of(e)},
        )

    def sub_copies(e, u):
        there = others - 1 - u
        to = {"sub": sub_of(u)}
        return (
            remote(
                own_units.at[e, core],
                far_units.at[there, e, core],
                sub_send_sem.at[0, u, e],
                sub_got_sem.at[0, there, e],
                to,
            ),
            remote(
                own_aff.at[e],
                far_aff.at[there, e],
                sub_send_sem.at[1, u, e],
                sub_got_sem.at[1, there, e],
                to,
            ),
        )

    def pair_copies(e):
        there = peers - 1 - e
        to = {"pairs": peer_of(e)}
        return (
            remote(
                send_units.at[e],
                got_units.at[there, core],
                pair_send_sem.at[0, e],
                pair_got_sem.at[0, there],
                to,
            ),
            remote(
                send_aff.at[e],
                got_aff.at[there],
                pair_send_sem.at[1, e],
                pair_got_sem.at[1, there],
                to,
            ),
        )

    def far_share(e, u, v):
        there = mates - 1 - v
        piece = far_units.at[u, e, core]
        return remote(
            piece,
            piece,
            far_send_sem.at[u, e, v],
            far_got_sem.at[u, e, there],
            {"feat": mate_of(v)},
        )

    def got_share(e, v):
        there = mates - 1 - v
        piece = got_units.at[e, core]
        return remote(
            piece,
            piece,
            share_send_sem.at[e, v],
            share_got_sem.at[e, there],
            {"feat": mate_of(v)},
        )

    def near_copy(e):
        there = peers - 1 - e
        return remote(
            near_send.at[e],
            near_got.at[there],
            near_send_sem.at[e],
            near_got_sem.at[there],
            {"pairs": peer_of(e)},
        )

    def back_copy(e, u):
        there = others - 1 - u
        return remote(
            back_send.at[u, e],
            back_got.at[there, e],
            back_send_sem.at[u, e],
            back_got_sem.at[there, e],
            {"sub": sub_of(u)},
        )

    fetches = [
        pltpu.make_async_copy(src, dst, fetch_sem.at[i])
        for i, (src, dst) in enumerate(
            [
                (table_hbm, table_ref),
                (owner_hbm, owner_ref),
                (counts_hbm, counts_ref),
                (vec_hbm, vec_ref),
                (aff_hbm, aff_ref),
            ]
        )
    ]
    for fetch in fetches:
        fetch.start()

    barrier = pltpu.get_barrier_semaphore()

    def greet_peer(e):
        pl.semaphore_signal(barrier, inc=1, device_id={"pairs": peer_of(e)}, device_id_type=MESH)

    def greet_sub(u):
        pl.semaphore_signal(barrier, inc=1, device_id={"sub": sub_of(u)}, device_id_type=MESH)

    loop(peers, greet_peer)
    def greet_mate(v):
        pl.semaphore_signal(barrier, inc=1, device_id={"feat": mate_of(v)}, device_id_type=MESH)

    loop(others, greet_sub)
    loop(mates, greet_mate)
    for fetch in fetches:
        fetch.wait()

    def fill_pair(e):
        send_units[e] = unit(vec_ref[asked_local(e), core])
        fill_aff(asked_local(e), send_aff, e)

    loop(peers, fill_pair)
    pl.semaphore_wait(barrier, peers + others + mates)

    loop(peers, lambda e: table_copy(e).start())

    def start_pair(e):
        for copy in pair_copies(e):
            copy.start()

    loop(peers, start_pair)

    loop(peers, lambda e: table_copy(peers - 1 - e).wait_recv())

    def start_own(e):
        own_units[e, core] = unit(vec_ref[own_local(e), core])
        fill_aff(own_local(e), own_aff, e)

        def send(u):
            for copy in sub_copies(e, u):
                copy.start()

        loop(others, send)

    loop(peers, start_own)

    def fill_rest(e):
        for v in range(mates):
            own_units[e, mate_of(v)] = unit(vec_ref[own_local(e), mate_of(v)])

    loop(peers, fill_rest)

    def count_step(b, found):
        at = owner_ref[b] - me * blocks
        return tuple(jnp.where(at == l, counts_ref[b], found[l]) for l in range(blocks))

    own_counts = fold(
        counts_ref.shape[0], count_step, (jnp.int32(0),) * blocks, unrolled=32
    )

    def share_far(e):
        for u in range(others):
            for copy in sub_copies(e, others - 1 - u):
                copy.wait_recv()
            for v in range(mates):
                far_share(e, u, v).start()

    def share_got(e):
        for copy in pair_copies(peers - 1 - e):
            copy.wait_recv()
        for v in range(mates):
            got_share(e, v).start()

    loop(peers, share_got)

    lane = lax.broadcasted_iota(jnp.int32, (height, rows), 1)

    def cut(aff, first_row, count):
        keep = first_row + lane < count
        full = jnp.concatenate(
            [aff.astype(jnp.float32), jnp.ones((height - cols, rows), jnp.float32)], axis=0
        )
        return jnp.where(keep, full, 0.0).astype(jnp.bfloat16)

    def tile(a_units, a_aug, b_units, b_aug):
        cosine = lax.dot_general(
            b_units, a_units, (((1,), (1,)), ((), ())), preferred_element_type=jnp.float32
        )
        rounded = jnp.exp(sharpness * (cosine - 1.0)).astype(jnp.bfloat16)
        near = lax.dot_general(
            a_aug, rounded, (((1,), (1,)), ((), ())), preferred_element_type=jnp.float32
        )
        back = jnp.dot(b_aug, rounded, preferred_element_type=jnp.float32)
        return near, back

    def live_counts(e):
        first, second = own_pair(e)
        live = second >= 0
        return (
            jnp.where(live, counts_ref[jnp.maximum(first, 0)], 0),
            jnp.where(live, counts_ref[jnp.maximum(second, 0)], 0),
        )

    def own_step(e):
        a_count, b_count = live_counts(e)
        a_aug = cut(own_aff[e], sub * rows, a_count)
        for v in range(mates):
            got_share(e, mates - 1 - v).wait_recv()
        near_sum[e], back_own[e] = tile(
            own_units[e].reshape(rows, width),
            a_aug,
            got_units[e].reshape(rows, width),
            cut(got_aff[e], sub * rows, b_count),
        )

    def far_step(e):
        a_count, b_count = live_counts(e)
        b_aug = cut(got_aff[e], sub * rows, b_count)
        near = near_sum[e]
        for u in range(others):
            a_aug = cut(far_aff[u, e], sub_of(u) * rows, a_count)
            for v in range(mates):
                far_share(e, u, mates - 1 - v).wait_recv()
            more, back = tile(
                far_units[u, e].reshape(rows, width),
                a_aug,
                got_units[e].reshape(rows, width),
                b_aug,
            )
            back_send[u, e] = back.astype(jnp.bfloat16)
            back_copy(e, u).start()
            near = near + more
        near_send[e] = near.astype(jnp.bfloat16)
        near_copy(e).start()

    loop(peers, own_step)
    if peers > 0:
        share_far(0)

    def far_turn(e):
        if isinstance(e, int):
            if e + 1 < peers:
                share_far(e + 1)
        else:

            @pl.when(e + 1 < peers)
            def _():
                share_far(e + 1)

        far_step(e)

    loop(peers, far_turn)

    def arrive(e):
        near_copy(peers - 1 - e).wait_recv()

        def back_in(u):
            back_copy(e, others - 1 - u).wait_recv()

        loop(others, back_in)

    loop(peers, arrive)

    column = lax.broadcasted_iota(jnp.int32, (cols, rows), 1)
    for l in range(blocks):

        def add(e, total, l=l):
            own, asked = own_pair(e), asked_pair(e)
            mine = (own[1] >= 0) & (own_local(e) == l)
            theirs = (asked[1] >= 0) & (asked_local(e) == l)
            part = back_own[e]
            for u in range(others):
                part = part + back_got[u, e].astype(jnp.float32)
            total = total + jnp.where(mine, part, 0.0)
            return total + jnp.where(theirs, near_got[e].astype(jnp.float32), 0.0)

        total = fold(peers, add, jnp.zeros((height, rows), jnp.float32))
        numer = aff_ref[l].astype(jnp.float32) + total[0:cols]
        denom = 1.0 + total[cols : cols + 1]
        keep = sub * rows + column < own_counts[l]
        out_ref[l] = jnp.where(keep, numer * (1.0 / denom), 0.0).astype(jnp.bfloat16)

    def sent(e):
        table_copy(e).wait_send()
        near_copy(e).wait_send()
        for copy in pair_copies(e):
            copy.wait_send()
        for v in range(mates):
            got_share(e, v).wait_send()

        def sub_sent(u):
            for v in range(mates):
                far_share(e, u, v).wait_send()
            back_copy(e, u).wait_send()
            for copy in sub_copies(e, u):
                copy.wait_send()

        loop(others, sub_sent)

    loop(peers, sent)


def on_device(vectors, affinity, counts, owner_map, pair_table):
    pair_count = lax.axis_size("pairs")
    sub_count = lax.axis_size("sub")
    core_count = lax.axis_size("feat")
    blocks, rows, width = vectors.shape
    cols = affinity.shape[2]
    height = cols + 16
    peers, others, mates = pair_count - 1, sub_count - 1, core_count - 1
    part = rows // core_count
    parts = (core_count, part, width)
    slots = pair_table.shape[0]
    table = pair_table.T
    half = jnp.bfloat16
    dma = pltpu.SemaphoreType.DMA
    vmem = pl.BlockSpec(memory_space=pltpu.VMEM)
    hbm = pl.BlockSpec(memory_space=pltpu.HBM)
    out = pl.pallas_call(
        functools.partial(kernel, pair_count, sub_count, core_count),
        out_shape=jax.ShapeDtypeStruct((blocks, cols, rows), half),
        in_specs=[hbm] * 5,
        out_specs=vmem,
        scratch_shapes=[
            pltpu.VMEM((blocks,) + parts, half),
            pltpu.VMEM((blocks, cols, rows), half),
            pltpu.SMEM(counts.shape, jnp.int32),
            pltpu.SMEM(owner_map.shape, jnp.int32),
            pltpu.SMEM((2, slots), jnp.int32),
            pltpu.VMEM((peers,) + parts, half),
            pltpu.VMEM((peers, cols, rows), half),
            pltpu.VMEM((others, peers) + parts, half),
            pltpu.VMEM((others, peers, cols, rows), half),
            pltpu.VMEM((peers, part, width), half),
            pltpu.VMEM((peers, cols, rows), half),
            pltpu.VMEM((peers,) + parts, half),
            pltpu.VMEM((peers, cols, rows), half),
            pltpu.VMEM((peers, height, rows), jnp.float32),
            pltpu.VMEM((peers, height, rows), half),
            pltpu.VMEM((peers, height, rows), half),
            pltpu.VMEM((peers, height, rows), jnp.float32),
            pltpu.VMEM((others, peers, height, rows), half),
            pltpu.VMEM((others, peers, height, rows), half),
            pltpu.SMEM((peers, 2, slots), jnp.int32),
            dma((5,)),
            dma((peers,)),
            dma((peers,)),
            dma((2, others, peers)),
            dma((2, others, peers)),
            dma((2, peers)),
            dma((2, peers)),
            dma((peers,)),
            dma((peers,)),
            dma((others, peers)),
            dma((others, peers)),
            dma((others, peers, mates)),
            dma((others, peers, mates)),
            dma((peers, mates)),
            dma((peers, mates)),
        ],
        compiler_params=pltpu.CompilerParams(
            collective_id=0, has_side_effects=True, vmem_limit_bytes=62 * 1024 * 1024
        ),
        name="pair_sums",
    )(
        vectors.reshape((blocks,) + parts),
        affinity.transpose(0, 2, 1),
        counts,
        owner_map,
        table,
    )
    return out.transpose(0, 2, 1)


def solution(mesh):
    in_specs = (
        P(("groups", "pairs"), "sub", None),
        P(("groups", "pairs"), "sub", "feat"),
        P("groups"),
        P("groups"),
        P(("groups", "pairs"), None),
    )
    out_specs = P(("groups", "pairs"), "sub", "feat")
    return jax.shard_map(
        on_device, mesh=mesh, in_specs=in_specs, out_specs=out_specs, check_vma=False
    )
```

```python
import functools

import jax
import jax.numpy as jnp
from jax import lax
from jax.experimental import pallas as pl
from jax.experimental.pallas import tpu as pltpu
from jax.sharding import PartitionSpec as P

sharpness = 8.0
MESH = pl.DeviceIdType.MESH


def loop(count, body, unrolled=4):
    if count <= unrolled:
        for i in range(count):
            body(i)
    else:

        def step(i, carry):
            body(i)
            return carry

        lax.fori_loop(0, count, step, 0)


def fold(count, body, start, unrolled=4):
    if count <= unrolled:
        for i in range(count):
            start = body(i, start)
        return start
    return lax.fori_loop(0, count, body, start)


def kernel(
    pair_count,
    sub_count,
    core_count,
    vec_hbm,
    aff_hbm,
    counts_hbm,
    owner_hbm,
    table_hbm,
    out_ref,
    vec_ref,
    aff_ref,
    counts_ref,
    owner_ref,
    table_ref,
    own_units,
    own_aff,
    far_units,
    far_aff,
    send_units,
    send_aff,
    got_units,
    got_aff,
    near_sum,
    near_send,
    near_got,
    back_own,
    back_send,
    back_got,
    tables,
    fetch_sem,
    tab_send_sem,
    tab_got_sem,
    sub_send_sem,
    sub_got_sem,
    pair_send_sem,
    pair_got_sem,
    near_send_sem,
    near_got_sem,
    back_send_sem,
    back_got_sem,
    far_send_sem,
    far_got_sem,
    share_send_sem,
    share_got_sem,
):
    me = lax.axis_index("pairs")
    sub = lax.axis_index("sub")
    core = lax.axis_index("feat")
    blocks, _, part, width = vec_ref.shape
    rows = part * core_count
    cols = aff_ref.shape[1]
    mates = core_count - 1
    height = back_own.shape[1]
    slots = table_ref.shape[1]
    peers = pair_count - 1
    others = sub_count - 1

    def peer_of(e):
        return lax.rem(me + e + 1, pair_count)

    def sub_of(u):
        return lax.rem(sub + u + 1, sub_count)

    def place(block):
        return owner_ref[jnp.maximum(block, 0)]

    def find(entry, target):
        def step(k, found):
            first, second = entry(0, k), entry(1, k)
            hit = (second >= 0) & (lax.div(place(second), jnp.int32(blocks)) == target)
            return jnp.where(hit, first, found[0]), jnp.where(hit, second, found[1])

        return fold(slots, step, (jnp.int32(-1), jnp.int32(-1)))

    def local_of(block):
        return lax.rem(place(block), jnp.int32(blocks))

    def mate_of(v):
        return lax.rem(core + v + 1, core_count)

    known = {}

    def once(name, e, work):
        if not isinstance(e, int):
            return work()
        if (name, e) not in known:
            known[name, e] = work()
        return known[name, e]

    def own_pair(e):
        return once("own", e, lambda: find(lambda i, k: tables[e, i, k], me)[::-1])

    def asked_pair(e):
        return once("asked", e, lambda: find(lambda i, k: table_ref[i, k], peer_of(e))[::-1])

    def own_local(e):
        return once("own at", e, lambda: local_of(own_pair(e)[0]))

    def asked_local(e):
        return once("asked at", e, lambda: local_of(asked_pair(e)[1]))

    def unit(floats):
        floats = floats.astype(jnp.float32)
        scale = lax.rsqrt(jnp.sum(floats * floats, axis=1, keepdims=True) + 1e-06)
        return (floats * scale).astype(jnp.bfloat16)

    def fill_aff(block, to_ref, e):
        to_ref[e] = aff_ref[block]

    def remote(src, dst, send_sem, got_sem, device):
        return pltpu.make_async_remote_copy(
            src_ref=src,
            dst_ref=dst,
            send_sem=send_sem,
            recv_sem=got_sem,
            device_id=device,
            device_id_type=MESH,
        )

    def table_copy(e):
        there = peers - 1 - e
        return remote(
            table_ref,
            tables.at[there],
            tab_send_sem.at[e],
            tab_got_sem.at[there],
            {"pairs": peer_of(e)},
        )

    def sub_copies(e, u):
        there = others - 1 - u
        to = {"sub": sub_of(u)}
        return (
            remote(
                own_units.at[e, core],
                far_units.at[there, e, core],
                sub_send_sem.at[0, u, e],
                sub_got_sem.at[0, there, e],
                to,
            ),
            remote(
                own_aff.at[e],
                far_aff.at[there, e],
                sub_send_sem.at[1, u, e],
                sub_got_sem.at[1, there, e],
                to,
            ),
        )

    def pair_copies(e):
        there = peers - 1 - e
        to = {"pairs": peer_of(e)}
        return (
            remote(
                send_units.at[e],
                got_units.at[there, core],
                pair_send_sem.at[0, e],
                pair_got_sem.at[0, there],
                to,
            ),
            remote(
                send_aff.at[e],
                got_aff.at[there],
                pair_send_sem.at[1, e],
                pair_got_sem.at[1, there],
                to,
            ),
        )

    def far_share(e, u, v):
        there = mates - 1 - v
        piece = far_units.at[u, e, core]
        return remote(
            piece,
            piece,
            far_send_sem.at[u, e, v],
            far_got_sem.at[u, e, there],
            {"feat": mate_of(v)},
        )

    def got_share(e, v):
        there = mates - 1 - v
        piece = got_units.at[e, core]
        return remote(
            piece,
            piece,
            share_send_sem.at[e, v],
            share_got_sem.at[e, there],
            {"feat": mate_of(v)},
        )

    def near_copy(e):
        there = peers - 1 - e
        return remote(
            near_send.at[e],
            near_got.at[there],
            near_send_sem.at[e],
            near_got_sem.at[there],
            {"pairs": peer_of(e)},
        )

    def back_copy(e, u):
        there = others - 1 - u
        return remote(
            back_send.at[u, e],
            back_got.at[there, e],
            back_send_sem.at[u, e],
            back_got_sem.at[there, e],
            {"sub": sub_of(u)},
        )

    fetches = [
        pltpu.make_async_copy(src, dst, fetch_sem.at[i])
        for i, (src, dst) in enumerate(
            [
                (table_hbm, table_ref),
                (owner_hbm, owner_ref),
                (counts_hbm, counts_ref),
                (vec_hbm, vec_ref),
                (aff_hbm, aff_ref),
            ]
        )
    ]
    for fetch in fetches:
        fetch.start()

    barrier = pltpu.get_barrier_semaphore()

    def greet_peer(e):
        pl.semaphore_signal(barrier, inc=1, device_id={"pairs": peer_of(e)}, device_id_type=MESH)

    def greet_sub(u):
        pl.semaphore_signal(barrier, inc=1, device_id={"sub": sub_of(u)}, device_id_type=MESH)

    loop(peers, greet_peer)
    def greet_mate(v):
        pl.semaphore_signal(barrier, inc=1, device_id={"feat": mate_of(v)}, device_id_type=MESH)

    loop(others, greet_sub)
    loop(mates, greet_mate)
    for fetch in fetches:
        fetch.wait()

    def fill_pair(e):
        send_units[e] = unit(vec_ref[asked_local(e), core])
        fill_aff(asked_local(e), send_aff, e)

    loop(peers, fill_pair)
    pl.semaphore_wait(barrier, peers + others + mates)

    loop(peers, lambda e: table_copy(e).start())

    def start_pair(e):
        for copy in pair_copies(e):
            copy.start()

    loop(peers, start_pair)

    loop(peers, lambda e: table_copy(peers - 1 - e).wait_recv())

    def start_own(e):
        own_units[e, core] = unit(vec_ref[own_local(e), core])
        fill_aff(own_local(e), own_aff, e)

        def send(u):
            for copy in sub_copies(e, u):
                copy.start()

        loop(others, send)

    loop(peers, start_own)

    def fill_rest(e):
        for v in range(mates):
            own_units[e, mate_of(v)] = unit(vec_ref[own_local(e), mate_of(v)])

    loop(peers, fill_rest)

    def count_step(b, found):
        at = owner_ref[b] - me * blocks
        return tuple(jnp.where(at == l, counts_ref[b], found[l]) for l in range(blocks))

    own_counts = fold(
        counts_ref.shape[0], count_step, (jnp.int32(0),) * blocks, unrolled=32
    )

    def share_far(e):
        for u in range(others):
            for copy in sub_copies(e, others - 1 - u):
                copy.wait_recv()
            for v in range(mates):
                far_share(e, u, v).start()

    def share_got(e):
        for copy in pair_copies(peers - 1 - e):
            copy.wait_recv()
        for v in range(mates):
            got_share(e, v).start()

    loop(peers, share_got)
    if peers > 0:
        share_far(0)

    lane = lax.broadcasted_iota(jnp.int32, (height, rows), 1)

    def cut(aff, first_row, count):
        keep = first_row + lane < count
        full = jnp.concatenate(
            [aff.astype(jnp.float32), jnp.ones((height - cols, rows), jnp.float32)], axis=0
        )
        return jnp.where(keep, full, 0.0).astype(jnp.bfloat16)

    def tile(a_units, a_aug, b_units, b_aug):
        cosine = lax.dot_general(
            b_units, a_units, (((1,), (1,)), ((), ())), preferred_element_type=jnp.float32
        )
        rounded = jnp.exp(sharpness * (cosine - 1.0)).astype(jnp.bfloat16)
        near = lax.dot_general(
            a_aug, rounded, (((1,), (1,)), ((), ())), preferred_element_type=jnp.float32
        )
        back = jnp.dot(b_aug, rounded, preferred_element_type=jnp.float32)
        return near, back

    def live_counts(e):
        first, second = own_pair(e)
        live = second >= 0
        return (
            jnp.where(live, counts_ref[jnp.maximum(first, 0)], 0),
            jnp.where(live, counts_ref[jnp.maximum(second, 0)], 0),
        )

    def own_step(e):
        a_count, b_count = live_counts(e)
        a_aug = cut(own_aff[e], sub * rows, a_count)
        for v in range(mates):
            got_share(e, mates - 1 - v).wait_recv()
        near_sum[e], back_own[e] = tile(
            own_units[e].reshape(rows, width),
            a_aug,
            got_units[e].reshape(rows, width),
            cut(got_aff[e], sub * rows, b_count),
        )

    def far_step(e):
        a_count, b_count = live_counts(e)
        b_aug = cut(got_aff[e], sub * rows, b_count)
        near = near_sum[e]
        for u in range(others):
            a_aug = cut(far_aff[u, e], sub_of(u) * rows, a_count)
            for v in range(mates):
                far_share(e, u, mates - 1 - v).wait_recv()
            more, back = tile(
                far_units[u, e].reshape(rows, width),
                a_aug,
                got_units[e].reshape(rows, width),
                b_aug,
            )
            back_send[u, e] = back.astype(jnp.bfloat16)
            back_copy(e, u).start()
            near = near + more
        near_send[e] = near.astype(jnp.bfloat16)
        near_copy(e).start()

    loop(peers, own_step)

    def far_turn(e):
        if isinstance(e, int):
            if e + 1 < peers:
                share_far(e + 1)
        else:

            @pl.when(e + 1 < peers)
            def _():
                share_far(e + 1)

        far_step(e)

    loop(peers, far_turn)

    def arrive(e):
        near_copy(peers - 1 - e).wait_recv()

        def back_in(u):
            back_copy(e, others - 1 - u).wait_recv()

        loop(others, back_in)

    loop(peers, arrive)

    column = lax.broadcasted_iota(jnp.int32, (cols, rows), 1)
    for l in range(blocks):

        def add(e, total, l=l):
            own, asked = own_pair(e), asked_pair(e)
            mine = (own[1] >= 0) & (own_local(e) == l)
            theirs = (asked[1] >= 0) & (asked_local(e) == l)
            part = back_own[e]
            for u in range(others):
                part = part + back_got[u, e].astype(jnp.float32)
            total = total + jnp.where(mine, part, 0.0)
            return total + jnp.where(theirs, near_got[e].astype(jnp.float32), 0.0)

        total = fold(peers, add, jnp.zeros((height, rows), jnp.float32))
        numer = aff_ref[l].astype(jnp.float32) + total[0:cols]
        denom = 1.0 + total[cols : cols + 1]
        keep = sub * rows + column < own_counts[l]
        out_ref[l] = jnp.where(keep, numer * (1.0 / denom), 0.0).astype(jnp.bfloat16)

    def sent(e):
        table_copy(e).wait_send()
        near_copy(e).wait_send()
        for copy in pair_copies(e):
            copy.wait_send()
        for v in range(mates):
            got_share(e, v).wait_send()

        def sub_sent(u):
            for v in range(mates):
                far_share(e, u, v).wait_send()
            back_copy(e, u).wait_send()
            for copy in sub_copies(e, u):
                copy.wait_send()

        loop(others, sub_sent)

    loop(peers, sent)


def on_device(vectors, affinity, counts, owner_map, pair_table):
    pair_count = lax.axis_size("pairs")
    sub_count = lax.axis_size("sub")
    core_count = lax.axis_size("feat")
    blocks, rows, width = vectors.shape
    cols = affinity.shape[2]
    height = cols + 16
    peers, others, mates = pair_count - 1, sub_count - 1, core_count - 1
    part = rows // core_count
    parts = (core_count, part, width)
    slots = pair_table.shape[0]
    table = pair_table.T
    half = jnp.bfloat16
    dma = pltpu.SemaphoreType.DMA
    vmem = pl.BlockSpec(memory_space=pltpu.VMEM)
    hbm = pl.BlockSpec(memory_space=pltpu.HBM)
    out = pl.pallas_call(
        functools.partial(kernel, pair_count, sub_count, core_count),
        out_shape=jax.ShapeDtypeStruct((blocks, cols, rows), half),
        in_specs=[hbm] * 5,
        out_specs=vmem,
        scratch_shapes=[
            pltpu.VMEM((blocks,) + parts, half),
            pltpu.VMEM((blocks, cols, rows), half),
            pltpu.SMEM(counts.shape, jnp.int32),
            pltpu.SMEM(owner_map.shape, jnp.int32),
            pltpu.SMEM((2, slots), jnp.int32),
            pltpu.VMEM((peers,) + parts, half),
            pltpu.VMEM((peers, cols, rows), half),
            pltpu.VMEM((others, peers) + parts, half),
            pltpu.VMEM((others, peers, cols, rows), half),
            pltpu.VMEM((peers, part, width), half),
            pltpu.VMEM((peers, cols, rows), half),
            pltpu.VMEM((peers,) + parts, half),
            pltpu.VMEM((peers, cols, rows), half),
            pltpu.VMEM((peers, height, rows), jnp.float32),
            pltpu.VMEM((peers, height, rows), half),
            pltpu.VMEM((peers, height, rows), half),
            pltpu.VMEM((peers, height, rows), jnp.float32),
            pltpu.VMEM((others, peers, height, rows), half),
            pltpu.VMEM((others, peers, height, rows), half),
            pltpu.SMEM((peers, 2, slots), jnp.int32),
            dma((5,)),
            dma((peers,)),
            dma((peers,)),
            dma((2, others, peers)),
            dma((2, others, peers)),
            dma((2, peers)),
            dma((2, peers)),
            dma((peers,)),
            dma((peers,)),
            dma((others, peers)),
            dma((others, peers)),
            dma((others, peers, mates)),
            dma((others, peers, mates)),
            dma((peers, mates)),
            dma((peers, mates)),
        ],
        compiler_params=pltpu.CompilerParams(
            collective_id=0, has_side_effects=True, vmem_limit_bytes=62 * 1024 * 1024
        ),
        name="pair_sums",
    )(
        vectors.reshape((blocks,) + parts),
        affinity.transpose(0, 2, 1),
        counts,
        owner_map,
        table,
    )
    return out.transpose(0, 2, 1)


def solution(mesh):
    in_specs = (
        P(("groups", "pairs"), "sub", None),
        P(("groups", "pairs"), "sub", "feat"),
        P("groups"),
        P("groups"),
        P(("groups", "pairs"), None),
    )
    out_specs = P(("groups", "pairs"), "sub", "feat")
    return jax.shard_map(
        on_device, mesh=mesh, in_specs=in_specs, out_specs=out_specs, check_vma=False
    )
```
